32 devices in a mesh: groups: 2 (over x), cols: 16 (over z, y, core).
Axes of the slice: x: 2, y: 2, z: 4, core: 2. Of those that a mesh axis runs over, the one named last changes fastest.
Arguments:
- state_field: bfloat16 [256, 256, 256], P(('groups', 'cols')), parts along dimension 0, may hold values from -6 to 6
- cotangent: bfloat16 [256, 256, 256], P(('groups', 'cols')), parts along dimension 0, may hold values from -6 to 6
- interp_blocks: bfloat16 [256, 7, 256, 256], P(('groups', 'cols')), parts along dimension 0, may hold values from -0.125 to 0.125
- upstream: int32 [256, 7], P(('groups', 'cols')), parts along dimension 0, may hold values from 0 to 127, as said below
- src_counts: int32 [256], P(('groups', 'cols')), parts along dimension 0, may hold values from 1 to 7, as said below
- w_in: bfloat16 [256, 512], replicated, may hold values from -0.375 to 0.375
- in_bias: float32 [512], replicated, may hold values from -4 to 4
- w_out: bfloat16 [512, 256], replicated, may hold values from -0.25 to 0.25
Outputs:
- grad_state: float32 [256, 256, 256], P(('groups', 'cols')), parts along dimension 0
- grad_w_in: float32 [512, 512], P('groups'), parts along dimension 0
- grad_w_out: float32 [1024, 256], P('groups'), parts along dimension 0
The draws below stay inside these ranges and needn't reach their ends.
There are 2 independent parts, one for each index of `groups`. The reference program is written for one: setup_inputs(seed, part) draws one part's arguments, and reference() takes and returns one part's arrays. A program takes and returns all parts, laid end to end along the dimension named above; an argument that names none is the same for every part. Nothing has to cross between parts.
Inputs may be any that keep to these rules, and one draw needn't show every extreme that they name: `upstream`: each entry of row t lies within 8 tiles of t in the periodic order of tiles, between t - 8 and t + 8 modulo 128; in tile 0 the first slot names tile 8. Slots at or past the tile's count are unused. `src_counts`: tile 0 has 7 live slots.
All inputs are finite; a program needn't handle non-finite values.
Results may differ from the reference program's by a relative error of at most 0.0047.
Values may be sent and summed in bfloat16 or wider, within the bound.
A program may use at most 128 MiB of HBM per device.

```python
import math
import jax
import jax.numpy as jnp
from jax import lax

FEAT = 256
HID = 512
TILE = 256
SRC = 7
TD = 8
TILES = 128
N_COLS = 16


def draw_upstream(key, part):
    key = jax.random.fold_in(key, 11)
    offsets = jax.random.randint(key, (TILES, SRC), -TD, TD + 1)
    offsets = offsets.at[0, 0].set(TD)
    tile_ids = jnp.arange(TILES, dtype=jnp.int32)[:, None]
    return ((tile_ids + offsets) % TILES).astype(jnp.int32)


def draw_src_counts(key, part):
    key = jax.random.fold_in(key, 23)
    counts_drawn = jax.random.randint(key, (TILES,), 1, SRC + 1)
    return counts_drawn.at[0].set(SRC).astype(jnp.int32)


def shard_levels(key, shape, pieces, smallest, largest):
    def one(dim, shards_of):
        steps = jax.random.uniform(jax.random.fold_in(jax.random.fold_in(key, 6), dim), (shards_of,), jnp.float32, smallest / len(pieces), largest / len(pieces))
        return jnp.repeat(jnp.exp(steps), shape[dim] // shards_of).reshape((-1,) + (1,) * (len(shape) - dim - 1))

    loudness = one(*pieces[0])
    for cut in pieces[1:]:
        loudness = loudness * one(*cut)
    return loudness


def normal_values(stream_key, extent, deviation, reach, pieces=(), kind=jnp.bfloat16):
    drawn = deviation * jax.random.normal(stream_key, extent, jnp.float32)
    if pieces:
        drawn = drawn * shard_levels(stream_key, extent, pieces, -0.22, 0.18)
    return jnp.clip(drawn, -reach, reach).astype(kind)


def setup_inputs(seed: int = 0, part: int = 0) -> dict:
    keys = jax.random.split(jax.random.key(seed), 9)
    own_keys = jax.random.split(jax.random.fold_in(keys[8], part), 9)
    return {
        "state_field": normal_values(own_keys[0], (TILES, TILE, FEAT), 1.0, 6.0, ((0, 16),)),
        "cotangent": normal_values(own_keys[1], (TILES, TILE, FEAT), 1.0, 6.0, ((0, 16),)),
        "interp_blocks": normal_values(own_keys[2], (TILES, SRC, TILE, TILE), (TILE * SRC) ** -0.5, 0.125, ((0, 16),)),
        "upstream": draw_upstream(jax.random.fold_in(jax.random.fold_in(keys[8], part), 71), part),
        "src_counts": draw_src_counts(jax.random.fold_in(jax.random.fold_in(keys[8], part), 71), part),
        "w_in": normal_values(keys[5], (FEAT, HID), FEAT ** -0.5, 0.375),
        "in_bias": normal_values(keys[6], (HID,), 1.0, 4.0, (), jnp.float32),
        "w_out": normal_values(keys[7], (HID, FEAT), HID ** -0.5, 0.25),
    }


def reference(state_field, cotangent, interp_blocks, upstream, src_counts, w_in, in_bias, w_out):
    live_slot = jnp.arange(SRC)[None, :] < src_counts[:, None]
    masked_blocks = interp_blocks * live_slot[:, :, None, None].astype(interp_blocks.dtype)
    upstream_cells = jnp.take(state_field, upstream.reshape(-1).astype(jnp.int32), axis=0).reshape(TILES, SRC, TILE, FEAT)
    transported = jnp.einsum('tkcd,tkdf->tcf', masked_blocks.astype(jnp.float32), upstream_cells.astype(jnp.float32)).astype(jnp.bfloat16)
    col_rows = transported.reshape(TILES * TILE, FEAT)
    pre_act = jnp.dot(col_rows, w_in, preferred_element_type=jnp.float32) + in_bias
    sigmoid_val = jax.nn.sigmoid(pre_act)
    hidden = (pre_act * sigmoid_val).astype(jnp.bfloat16)
    cot_rows = cotangent.reshape(TILES * TILE, FEAT)
    back_grad = jnp.dot(cot_rows, w_out.T, preferred_element_type=jnp.float32)
    pre_grad = (back_grad * sigmoid_val * (1.0 + pre_act * (1.0 - sigmoid_val))).astype(jnp.bfloat16)
    upstream_grad = (cot_rows.astype(jnp.float32) + jnp.dot(pre_grad, w_in.T, preferred_element_type=jnp.float32)).astype(jnp.bfloat16)
    norm_scale = 1.0 / math.sqrt(TILES * TILE)
    grad_w_in = jnp.dot(col_rows.T, pre_grad, preferred_element_type=jnp.float32) * norm_scale
    grad_w_out = jnp.dot(hidden.T, cot_rows, preferred_element_type=jnp.float32) * norm_scale
    upstream_grad = upstream_grad.reshape(TILES, TILE, FEAT)
    products = jnp.einsum('tkcd,tcf->tkdf', masked_blocks.astype(jnp.float32), upstream_grad.astype(jnp.float32))
    products = products.reshape(TILES * SRC, TILE, FEAT)
    target = upstream.reshape(-1).astype(jnp.int32)
    source_block = jnp.arange(TILES * SRC, dtype=jnp.int32) // SRC // TD
    block_gap = (target // TD - source_block + 1) % N_COLS - 1
    grad_state = jnp.zeros((TILES, TILE, FEAT), products.dtype)
    for offset in (-1, 0, 1):
        chosen = (block_gap == offset)[:, None, None]
        block_sum = jax.ops.segment_sum(jnp.where(chosen, products, 0.0), target, num_segments=TILES)
        rounded = lax.optimization_barrier(block_sum.astype(jnp.bfloat16))
        grad_state = grad_state + rounded.astype(products.dtype)
    return (grad_state, grad_w_in, grad_w_out)
```

```python
import functools

import jax
import jax.numpy as jnp
from jax import lax
from jax.experimental import pallas as pl
from jax.experimental.pallas import tpu as pltpu
from jax.sharding import PartitionSpec as P

F32 = jnp.float32
BF16 = jnp.bfloat16
MESH = pl.DeviceIdType.MESH
TN = (((0,), (0,)), ((), ()))
NT = (((1,), (1,)), ((), ()))


def mm(a, b):
    return jnp.dot(a, b, preferred_element_type=F32)


def kernel(
    n,
    table,
    state,
    cot_hbm,
    blocks_hbm,
    w_in,
    bias,
    w_out,
    out_state,
    out_w,
    near,
    land,
    blocks,
    cot,
    sums,
    xs,
    hs,
    pgs,
    far_out,
    sib_out,
    far_in,
    sib_in,
    out_buf,
    acc,
    core_in,
    z_out,
    z_in,
    y_out,
    y_in,
    gw,
    local_sem,
    blocks_sem,
    out_sem,
    far_ssem,
    far_rsem,
    sib_ssem,
    sib_rsem,
    cfar_ssem,
    cfar_rsem,
    csib_ssem,
    csib_rsem,
    core_sem,
    z_ssem,
    z_rsem,
    y_sem,
    g_ssem,
    g_rsem,
    last_sem,
):
    td, slots = blocks.shape[0], blocks.shape[1]
    nz = z_out.shape[0]
    rz = z_out.shape[1]
    pairs = td * slots
    me = lax.axis_index("cols")
    par = lax.rem(me, 2)
    sib = me + 1 - 2 * par
    far = lax.rem(me - 1 + 2 * par + n, n)
    zi = me // 4
    low = lax.rem(me, 4)
    y_mate = me + 2 - 4 * (low // 2)
    z_mates = [lax.rem(zi + d, nz) * 4 + low for d in range(1, nz)]

    def tile_at(s):
        return par * s + (1 - par) * (td - 1 - s)

    def send(src, dst, ssem, rsem, to):
        return pltpu.make_async_remote_copy(
            src_ref=src,
            dst_ref=dst,
            send_sem=ssem,
            recv_sem=rsem,
            device_id={"cols": to},
            device_id_type=MESH,
        )

    own_copy = pltpu.make_async_copy(state, near.at[pl.ds(td, td)], local_sem.at[0])
    own_copy.start()
    cot_copy = pltpu.make_async_copy(cot_hbm, cot, local_sem.at[1])
    cot_copy.start()

    def load_blocks(s):
        t = tile_at(s)
        return pltpu.make_async_copy(blocks_hbm.at[t], blocks.at[t], blocks_sem.at[s])

    for s in range(td):
        load_blocks(s).start()

    barrier = pltpu.get_barrier_semaphore()
    mates = [sib, far, y_mate] + z_mates
    for mate in mates:
        pl.semaphore_signal(barrier, inc=1, device_id={"cols": mate}, device_id_type=MESH)
    pl.semaphore_wait(barrier, len(mates))

    def far_state(s):
        t = tile_at(td - 1 - s)
        return send(state.at[t], land.at[s], far_ssem.at[s], far_rsem.at[s], far)

    for s in range(td):
        far_state(s).start()
    sib_state = send(state, near.at[pl.ds(2 * td * par, td)], sib_ssem, sib_rsem, sib)
    sib_state.start()

    near[3 * td] = jnp.zeros(near.shape[1:], BF16)
    sums[pairs] = jnp.zeros(sums.shape[1:], F32)
    own_copy.wait()
    cot_copy.wait()
    sib_state.wait()
    far_base = 2 * td * par
    sib_base = 2 * td * (1 - par)

    def step(s, carry):
        t = tile_at(s)
        far_state(s).wait()
        near[far_base + t] = land[s]
        load_blocks(s).wait()
        moved = mm(blocks[t, 0], near[table[s * slots]])
        for k in range(1, slots):
            moved += mm(blocks[t, k], near[table[s * slots + k]])
        moved = moved.astype(BF16)
        xs[t] = moved
        pre = mm(moved, w_in[...]) + bias[...]
        sig = jax.nn.sigmoid(pre)
        hs[t] = (pre * sig).astype(BF16)
        here = cot[t]
        back = lax.dot_general(here, w_out[...], NT, preferred_element_type=F32)
        pg = (back * sig * (1.0 + pre * (1.0 - sig))).astype(BF16)
        pgs[t] = pg
        up = here.astype(F32) + lax.dot_general(pg, w_in[...], NT, preferred_element_type=F32)
        up_t = jnp.transpose(up).astype(BF16)
        for k in range(slots):
            p = s * slots + k
            sums[p] = mm(up_t, blocks[t, k]) + sums[table[pairs + p]]
        return carry

    lax.fori_loop(0, td, step, 0)

    def far_part(i):
        return send(far_out.at[i], far_in.at[i], cfar_ssem.at[i], cfar_rsem.at[i], far)

    def sib_part(i):
        return send(sib_out.at[i], sib_in.at[i], csib_ssem.at[i], csib_rsem.at[i], sib)

    def post_far(i, carry):
        far_out[i] = sums[table[2 * pairs + far_base + i]].astype(BF16)
        far_part(i).start()
        return carry

    lax.fori_loop(0, td, post_far, 0)

    def post_sib(i, carry):
        sib_out[i] = sums[table[2 * pairs + sib_base + i]].astype(BF16)
        sib_part(i).start()
        return carry

    lax.fori_loop(0, td, post_sib, 0)

    acc[...] = jnp.zeros_like(acc)

    def weights(t, carry):
        acc[0] += lax.dot_general(xs[t], pgs[t], TN, preferred_element_type=F32)
        acc[1] += lax.dot_general(cot[t], hs[t], TN, preferred_element_type=F32)
        return carry

    lax.fori_loop(0, td, weights, 0)

    core_copy = send(acc.at[1 - par], core_in, core_sem.at[0], core_sem.at[1], sib)
    core_copy.start()
    core_copy.wait()
    for z in range(nz):
        rows = pl.ds(z * rz, rz)
        piece = acc[par, rows] + core_in[rows]
        acc[par, rows] = piece
        z_out[z] = piece.astype(BF16)
    z_copies = []
    for d in range(1, nz):
        there = lax.rem(zi + d, nz)
        z_copies.append(
            send(z_out.at[there], z_in.at[d - 1], z_ssem.at[d - 1], z_rsem.at[d - 1], z_mates[d - 1])
        )
        z_copies[-1].start()
    total = acc[par, pl.ds(pl.multiple_of(zi * rz, rz), rz)]
    for d in range(1, nz):
        z_copies[d - 1].wait()
        total += z_in[d - 1].astype(F32)
    y_out[...] = total
    y_copy = send(y_out, y_in, y_sem.at[0], y_sem.at[1], y_mate)
    y_copy.start()
    y_copy.wait()
    gw[par, zi] = (y_out[...] + y_in[...]).astype(BF16)
    g_copies = []
    for d in range(1, nz):
        g_copies.append(
            send(gw.at[par, zi], gw.at[par, zi], g_ssem.at[d - 1], g_rsem.at[d - 1], z_mates[d - 1])
        )
        g_copies[-1].start()
    for g_copy in g_copies:
        g_copy.wait()
    last_copy = send(gw.at[par], gw.at[par], last_sem.at[0], last_sem.at[1], sib)
    last_copy.start()

    def out_copy(i):
        return pltpu.make_async_copy(out_buf.at[i], out_state.at[i], out_sem.at[i])

    def finish(i, carry):
        own = sums[table[2 * pairs + td + i]].astype(BF16).astype(F32)
        sib_part(i).wait()
        far_part(i).wait()
        whole = own + sib_in[i].astype(F32) + far_in[i].astype(F32)
        out_buf[i] = jnp.transpose(whole)
        out_copy(i).start()
        return carry

    lax.fori_loop(0, td, finish, 0)
    last_copy.wait()
    w_copy = pltpu.make_async_copy(gw, out_w, local_sem.at[2])
    w_copy.start()
    for i in range(td):
        out_copy(i).wait()
    w_copy.wait()


def exchange(n, table, state, cotangent, blocks, w_in, bias, w_out):
    td, slots, cols, _ = blocks.shape
    feat = state.shape[2]
    hid = w_in.shape[1]
    nz = n // 4
    rz = feat // nz
    dma = pltpu.SemaphoreType.DMA
    vmem = pl.BlockSpec(memory_space=pltpu.VMEM)
    hbm = pl.BlockSpec(memory_space=pl.ANY)
    return pl.pallas_call(
        functools.partial(kernel, n),
        out_shape=(
            jax.ShapeDtypeStruct((td, cols, feat), F32),
            jax.ShapeDtypeStruct((2, nz, rz, hid), BF16),
        ),
        in_specs=[pl.BlockSpec(memory_space=pltpu.SMEM), hbm, hbm, hbm, vmem, vmem, vmem],
        out_specs=(hbm, hbm),
        scratch_shapes=[
            pltpu.VMEM((3 * td + 1, cols, feat), BF16),
            pltpu.VMEM((td, cols, feat), BF16),
            pltpu.VMEM((td, slots, cols, cols), BF16),
            pltpu.VMEM((td, cols, feat), BF16),
            pltpu.VMEM((td * slots + 1, feat, cols), F32),
            pltpu.VMEM((td, cols, feat), BF16),
            pltpu.VMEM((td, cols, hid), BF16),
            pltpu.VMEM((td, cols, hid), BF16),
            pltpu.VMEM((td, feat, cols), BF16),
            pltpu.VMEM((td, feat, cols), BF16),
            pltpu.VMEM((td, feat, cols), BF16),
            pltpu.VMEM((td, feat, cols), BF16),
            pltpu.VMEM((td, cols, feat), F32),
            pltpu.VMEM((2, feat, hid), F32),
            pltpu.VMEM((feat, hid), F32),
            pltpu.VMEM((nz, rz, hid), BF16),
            pltpu.VMEM((nz - 1, rz, hid), BF16),
            pltpu.VMEM((rz, hid), F32),
            pltpu.VMEM((rz, hid), F32),
            pltpu.VMEM((2, nz, rz, hid), BF16),
            dma((3,)),
            dma((td,)),
            dma((td,)),
            dma((td,)),
            dma((td,)),
            dma,
            dma,
            dma((td,)),
            dma((td,)),
            dma((td,)),
            dma((td,)),
            dma((2,)),
            dma((nz - 1,)),
            dma((nz - 1,)),
            dma((2,)),
            dma((nz - 1,)),
            dma((nz - 1,)),
            dma((2,)),
        ],
        compiler_params=pltpu.CompilerParams(
            collective_id=0, has_side_effects=True, vmem_limit_bytes=56 * 1024 * 1024
        ),
    )(table, state, cotangent, blocks, w_in, bias, w_out)


def per_device(state_field, cotangent, interp_blocks, upstream, src_counts, w_in, in_bias, w_out):
    td, cols, feat = state_field.shape
    slots = upstream.shape[1]
    n = lax.axis_size("cols")
    tile_total = td * n
    pairs = td * slots
    me = lax.axis_index("cols")
    live = jnp.arange(slots)[None, :] < src_counts[:, None]
    local = (upstream - me * td + td) % tile_total
    marked = jnp.where(live, local, -1)
    marked = jnp.where(me % 2 == 0, jnp.flip(marked, 0), marked).reshape(-1)
    order = jnp.arange(pairs, dtype=jnp.int32)
    same = (marked[:, None] == marked[None, :]) & (order[None, :] < order[:, None])
    before = jnp.max(jnp.where(same & (marked[:, None] >= 0), order[None, :], -1), axis=1)
    targets = jnp.arange(3 * td, dtype=jnp.int32)
    last = jnp.max(jnp.where(targets[:, None] == marked[None, :], order[None, :], -1), axis=1)
    table = jnp.concatenate(
        [
            jnp.where(marked < 0, 3 * td, marked),
            jnp.where(before < 0, pairs, before),
            jnp.where(last < 0, pairs, last),
        ]
    ).astype(jnp.int32)
    grad_state, gw = exchange(
        n, table, state_field, cotangent, interp_blocks, w_in, in_bias[None, :], w_out
    )
    norm_scale = 1.0 / jnp.sqrt(F32(tile_total * cols))
    hid = w_in.shape[1]
    grad_w_in = gw[0].reshape(feat, hid).astype(F32) * norm_scale
    grad_w_out = gw[1].reshape(feat, hid).astype(F32).T * norm_scale
    return (grad_state, grad_w_in, grad_w_out)


def solution(mesh):
    placed = (
        P(("groups", "cols"), None, None),
        P(("groups", "cols"), None, None),
        P(("groups", "cols"), None, None, None),
        P(("groups", "cols"), None),
        P(("groups", "cols")),
        P(),
        P(),
        P(),
    )
    return jax.shard_map(
        per_device,
        mesh=mesh,
        in_specs=placed,
        out_specs=(P(("groups", "cols"), None, None), P("groups", None), P("groups", None)),
        check_vma=False,
    )
```

```python
import functools

import jax
import jax.numpy as jnp
from jax import lax
from jax.experimental import pallas as pl
from jax.experimental.pallas import tpu as pltpu
from jax.sharding import PartitionSpec as P

F32 = jnp.float32
BF16 = jnp.bfloat16
MESH = pl.DeviceIdType.MESH
TN = (((0,), (0,)), ((), ()))
NT = (((1,), (1,)), ((), ()))


def mm(a, b):
    return jnp.dot(a, b, preferred_element_type=F32)


def kernel(
    n,
    table,
    state,
    cot_hbm,
    blocks_hbm,
    w_in,
    bias,
    w_out,
    out_state,
    out_w_in,
    out_w_out,
    near,
    land,
    blocks,
    cot,
    sums,
    xs,
    hs,
    pgs,
    far_out,
    sib_out,
    far_in,
    sib_in,
    out_buf,
    acc,
    core_in,
    z_out,
    z_in,
    y_out,
    y_in,
    gw,
    turned,
    local_sem,
    blocks_sem,
    out_sem,
    far_ssem,
    far_rsem,
    sib_ssem,
    sib_rsem,
    cfar_ssem,
    cfar_rsem,
    csib_ssem,
    csib_rsem,
    core_sem,
    z_ssem,
    z_rsem,
    y_sem,
    g_ssem,
    g_rsem,
    last_sem,
):
    td, slots = blocks.shape[0], blocks.shape[1]
    nz = z_out.shape[0]
    rz = z_out.shape[1]
    pairs = td * slots
    me = lax.axis_index("cols")
    par = lax.rem(me, 2)
    sib = me + 1 - 2 * par
    far = lax.rem(me - 1 + 2 * par + n, n)
    zi = me // 4
    low = lax.rem(me, 4)
    y_mate = me + 2 - 4 * (low // 2)
    z_mates = [lax.rem(zi + d, nz) * 4 + low for d in range(1, nz)]

    def tile_at(s):
        return par * s + (1 - par) * (td - 1 - s)

    def send(src, dst, ssem, rsem, to):
        return pltpu.make_async_remote_copy(
            src_ref=src,
            dst_ref=dst,
            send_sem=ssem,
            recv_sem=rsem,
            device_id={"cols": to},
            device_id_type=MESH,
        )

    own_copy = pltpu.make_async_copy(state, near.at[pl.ds(td, td)], local_sem.at[0])
    own_copy.start()
    cot_copy = pltpu.make_async_copy(cot_hbm, cot, local_sem.at[1])
    cot_copy.start()

    def load_blocks(s):
        t = tile_at(s)
        return pltpu.make_async_copy(blocks_hbm.at[t], blocks.at[t], blocks_sem.at[s])

    for s in range(td):
        load_blocks(s).start()

    barrier = pltpu.get_barrier_semaphore()
    mates = [sib, far, y_mate] + z_mates
    for mate in mates:
        pl.semaphore_signal(barrier, inc=1, device_id={"cols": mate}, device_id_type=MESH)
    pl.semaphore_wait(barrier, len(mates))

    def far_state(s):
        t = tile_at(td - 1 - s)
        return send(state.at[t], land.at[s], far_ssem.at[s], far_rsem.at[s], far)

    for s in range(td):
        far_state(s).start()
    sib_state = send(state, near.at[pl.ds(2 * td * par, td)], sib_ssem, sib_rsem, sib)
    sib_state.start()

    near[3 * td] = jnp.zeros(near.shape[1:], BF16)
    sums[pairs] = jnp.zeros(sums.shape[1:], F32)
    own_copy.wait()
    cot_copy.wait()
    sib_state.wait()
    far_base = 2 * td * par
    sib_base = 2 * td * (1 - par)

    acc[...] = jnp.zeros_like(acc)

    def weights(t):
        acc[0] += lax.dot_general(xs[t], pgs[t], TN, preferred_element_type=F32)
        acc[1] += lax.dot_general(cot[t], hs[t], TN, preferred_element_type=F32)

    def step(s, carry):
        t = tile_at(s)

        @pl.when(s > 0)
        def _():
            weights(tile_at(s - 1))

        far_state(s).wait()
        near[far_base + t] = land[s]
        load_blocks(s).wait()
        moved = mm(blocks[t, 0], near[table[s * slots]])
        for k in range(1, slots):
            moved += mm(blocks[t, k], near[table[s * slots + k]])
        moved = moved.astype(BF16)
        xs[t] = moved
        pre = mm(moved, w_in[...]) + bias[...]
        sig = jax.nn.sigmoid(pre)
        hs[t] = (pre * sig).astype(BF16)
        here = cot[t]
        back = lax.dot_general(here, w_out[...], NT, preferred_element_type=F32)
        pg = (back * sig * (1.0 + pre * (1.0 - sig))).astype(BF16)
        pgs[t] = pg
        up = here.astype(F32) + lax.dot_general(pg, w_in[...], NT, preferred_element_type=F32)
        up_t = jnp.transpose(up).astype(BF16)
        for k in range(slots):
            p = s * slots + k
            sums[p] = mm(up_t, blocks[t, k]) + sums[table[pairs + p]]
        return carry

    lax.fori_loop(0, td, step, 0)

    def far_part(i):
        return send(far_out.at[i], far_in.at[i], cfar_ssem.at[i], cfar_rsem.at[i], far)

    def sib_part(i):
        return send(sib_out.at[i], sib_in.at[i], csib_ssem.at[i], csib_rsem.at[i], sib)

    def post_far(i, carry):
        far_out[i] = sums[table[2 * pairs + far_base + i]].astype(BF16)
        far_part(i).start()
        return carry

    def post_sib(i, carry):
        sib_out[i] = sums[table[2 * pairs + sib_base + i]].astype(BF16)
        sib_part(i).start()
        return carry

    cuts = [0, td // 4, td // 2, td // 2 + td // 8, td - td // 4, td]
    lax.fori_loop(cuts[0], cuts[1], post_far, 0)
    weights(tile_at(td - 1))
    core_copy = send(acc.at[1 - par], core_in, core_sem.at[0], core_sem.at[1], sib)
    core_copy.start()
    lax.fori_loop(0, td, post_sib, 0)
    core_copy.wait()
    for z in range(nz):
        rows = pl.ds(z * rz, rz)
        piece = acc[par, rows] + core_in[rows]
        acc[par, rows] = piece
        z_out[z] = piece.astype(BF16)
    z_copies = []
    for d in range(1, nz):
        there = lax.rem(zi + d, nz)
        z_copies.append(
            send(z_out.at[there], z_in.at[d - 1], z_ssem.at[d - 1], z_rsem.at[d - 1], z_mates[d - 1])
        )
        z_copies[-1].start()
    lax.fori_loop(cuts[1], cuts[2], post_far, 0)
    total = acc[par, pl.ds(pl.multiple_of(zi * rz, rz), rz)]
    for d in range(1, nz):
        z_copies[d - 1].wait()
        total += z_in[d - 1].astype(F32)
    y_out[...] = total.astype(BF16)
    y_copy = send(y_out, y_in, y_sem.at[0], y_sem.at[1], y_mate)
    y_copy.start()
    lax.fori_loop(cuts[2], cuts[3], post_far, 0)
    y_copy.wait()
    gw[par, zi] = (y_out[...].astype(F32) + y_in[...].astype(F32)).astype(BF16)
    g_copies = []
    for d in range(1, nz):
        g_copies.append(
            send(gw.at[par, zi], gw.at[par, zi], g_ssem.at[d - 1], g_rsem.at[d - 1], z_mates[d - 1])
        )
        g_copies[-1].start()
    lax.fori_loop(cuts[3], cuts[4], post_far, 0)
    for g_copy in g_copies:
        g_copy.wait()
    last_copy = send(gw.at[par], gw.at[par], last_sem.at[0], last_sem.at[1], sib)
    last_copy.start()
    lax.fori_loop(cuts[4], cuts[5], post_far, 0)

    def out_copy(i):
        return pltpu.make_async_copy(out_buf.at[i], out_state.at[i], out_sem.at[i])

    def finish(i, carry):
        own = sums[table[2 * pairs + td + i]].astype(BF16).astype(F32)
        sib_part(i).wait()
        far_part(i).wait()
        whole = own + sib_in[i].astype(F32) + far_in[i].astype(F32)
        out_buf[i] = jnp.transpose(whole)
        out_copy(i).start()
        return carry

    lax.fori_loop(0, td, finish, 0)
    last_copy.wait()
    feat, hid = w_in.shape
    w_in_copy = pltpu.make_async_copy(gw.at[0], out_w_in, local_sem.at[2])
    w_in_copy.start()
    turned[...] = jnp.transpose(gw[1].reshape(feat, hid).astype(F32)).astype(BF16)
    w_out_copy = pltpu.make_async_copy(turned, out_w_out, local_sem.at[0])
    w_out_copy.start()
    for i in range(td):
        out_copy(i).wait()
    w_in_copy.wait()
    w_out_copy.wait()


def exchange(n, table, state, cotangent, blocks, w_in, bias, w_out):
    td, slots, cols, _ = blocks.shape
    feat = state.shape[2]
    hid = w_in.shape[1]
    nz = n // 4
    rz = feat // nz
    dma = pltpu.SemaphoreType.DMA
    vmem = pl.BlockSpec(memory_space=pltpu.VMEM)
    hbm = pl.BlockSpec(memory_space=pl.ANY)
    return pl.pallas_call(
        functools.partial(kernel, n),
        out_shape=(
            jax.ShapeDtypeStruct((td, cols, feat), F32),
            jax.ShapeDtypeStruct((nz, rz, hid), BF16),
            jax.ShapeDtypeStruct((hid, feat), BF16),
        ),
        in_specs=[pl.BlockSpec(memory_space=pltpu.SMEM), hbm, hbm, hbm, vmem, vmem, vmem],
        out_specs=(hbm, hbm, hbm),
        scratch_shapes=[
            pltpu.VMEM((3 * td + 1, cols, feat), BF16),
            pltpu.VMEM((td, cols, feat), BF16),
            pltpu.VMEM((td, slots, cols, cols), BF16),
            pltpu.VMEM((td, cols, feat), BF16),
            pltpu.VMEM((td * slots + 1, feat, cols), F32),
            pltpu.VMEM((td, cols, feat), BF16),
            pltpu.VMEM((td, cols, hid), BF16),
            pltpu.VMEM((td, cols, hid), BF16),
            pltpu.VMEM((td, feat, cols), BF16),
            pltpu.VMEM((td, feat, cols), BF16),
            pltpu.VMEM((td, feat, cols), BF16),
            pltpu.VMEM((td, feat, cols), BF16),
            pltpu.VMEM((td, cols, feat), F32),
            pltpu.VMEM((2, feat, hid), F32),
            pltpu.VMEM((feat, hid), F32),
            pltpu.VMEM((nz, rz, hid), BF16),
            pltpu.VMEM((nz - 1, rz, hid), BF16),
            pltpu.VMEM((rz, hid), BF16),
            pltpu.VMEM((rz, hid), BF16),
            pltpu.VMEM((2, nz, rz, hid), BF16),
            pltpu.VMEM((hid, feat), BF16),
            dma((3,)),
            dma((td,)),
            dma((td,)),
            dma((td,)),
            dma((td,)),
            dma,
            dma,
            dma((td,)),
            dma((td,)),
            dma((td,)),
            dma((td,)),
            dma((2,)),
            dma((nz - 1,)),
            dma((nz - 1,)),
            dma((2,)),
            dma((nz - 1,)),
            dma((nz - 1,)),
            dma((2,)),
        ],
        compiler_params=pltpu.CompilerParams(
            collective_id=0, has_side_effects=True, vmem_limit_bytes=56 * 1024 * 1024
        ),
    )(table, state, cotangent, blocks, w_in, bias, w_out)


def per_device(state_field, cotangent, interp_blocks, upstream, src_counts, w_in, in_bias, w_out):
    td, cols, feat = state_field.shape
    slots = upstream.shape[1]
    n = lax.axis_size("cols")
    tile_total = td * n
    pairs = td * slots
    me = lax.axis_index("cols")
    live = jnp.arange(slots)[None, :] < src_counts[:, None]
    local = (upstream - me * td + td) % tile_total
    marked = jnp.where(live, local, -1)
    marked = jnp.where(me % 2 == 0, jnp.flip(marked, 0), marked).reshape(-1)
    order = jnp.arange(pairs, dtype=jnp.int32)
    same = (marked[:, None] == marked[None, :]) & (order[None, :] < order[:, None])
    before = jnp.max(jnp.where(same & (marked[:, None] >= 0), order[None, :], -1), axis=1)
    targets = jnp.arange(3 * td, dtype=jnp.int32)
    last = jnp.max(jnp.where(targets[:, None] == marked[None, :], order[None, :], -1), axis=1)
    table = jnp.concatenate(
        [
            jnp.where(marked < 0, 3 * td, marked),
            jnp.where(before < 0, pairs, before),
            jnp.where(last < 0, pairs, last),
        ]
    ).astype(jnp.int32)
    grad_state, gw_in, gw_out = exchange(
        n, table, state_field, cotangent, interp_blocks, w_in, in_bias[None, :], w_out
    )
    norm_scale = 1.0 / jnp.sqrt(F32(tile_total * cols))
    hid = w_in.shape[1]
    grad_w_in = gw_in.reshape(feat, hid).astype(F32) * norm_scale
    grad_w_out = gw_out.astype(F32) * norm_scale
    return (grad_state, grad_w_in, grad_w_out)


def solution(mesh):
    placed = (
        P(("groups", "cols"), None, None),
        P(("groups", "cols"), None, None),
        P(("groups", "cols"), None, None, None),
        P(("groups", "cols"), None),
        P(("groups", "cols")),
        P(),
        P(),
        P(),
    )
    return jax.shard_map(
        per_device,
        mesh=mesh,
        in_specs=placed,
        out_specs=(P(("groups", "cols"), None, None), P("groups", None), P("groups", None)),
        check_vma=False,
    )
```

```python
import functools
import math

import jax
import jax.numpy as jnp
from jax import lax
from jax.experimental import pallas as pl
from jax.experimental.pallas import tpu as pltpu
from jax.sharding import PartitionSpec as P

F32 = jnp.float32
BF16 = jnp.bfloat16
MESH = pl.DeviceIdType.MESH
TN = (((0,), (0,)), ((), ()))
NT = (((1,), (1,)), ((), ()))


def mm(a, b):
    return jnp.dot(a, b, preferred_element_type=F32)


def kernel(
    n,
    table,
    state,
    cot_hbm,
    blocks_hbm,
    w_in,
    bias,
    w_out,
    out_state,
    out_w_in,
    out_w_out,
    near,
    land,
    blocks,
    cot,
    sums,
    xs,
    hs,
    pgs,
    far_out,
    sib_out,
    far_in,
    sib_in,
    out_buf,
    acc,
    core_in,
    z_out,
    z_in,
    y_out,
    y_in,
    gw,
    turned,
    local_sem,
    blocks_sem,
    out_sem,
    far_ssem,
    far_rsem,
    sib_ssem,
    sib_rsem,
    cfar_ssem,
    cfar_rsem,
    csib_ssem,
    csib_rsem,
    core_sem,
    z_ssem,
    z_rsem,
    y_sem,
    g_ssem,
    g_rsem,
    last_sem,
    turn_sem,
):
    td, slots = blocks.shape[0], blocks.shape[1]
    nz = z_out.shape[0]
    rz = z_out.shape[1]
    pairs = td * slots
    me = lax.axis_index("cols")
    par = lax.rem(me, 2)
    sib = me + 1 - 2 * par
    far = lax.rem(me - 1 + 2 * par + n, n)
    norm_scale = 1.0 / math.sqrt(n * td * blocks.shape[2])
    zi = me // 4
    low = lax.rem(me, 4)
    y_mate = me + 2 - 4 * (low // 2)
    z_mates = [lax.rem(zi + d, nz) * 4 + low for d in range(1, nz)]

    def tile_at(s):
        return par * s + (1 - par) * (td - 1 - s)

    def send(src, dst, ssem, rsem, to):
        return pltpu.make_async_remote_copy(
            src_ref=src,
            dst_ref=dst,
            send_sem=ssem,
            recv_sem=rsem,
            device_id={"cols": to},
            device_id_type=MESH,
        )

    own_copy = pltpu.make_async_copy(state, near.at[pl.ds(td, td)], local_sem.at[0])
    own_copy.start()
    cot_copy = pltpu.make_async_copy(cot_hbm, cot, local_sem.at[1])
    cot_copy.start()

    def load_blocks(s):
        t = tile_at(s)
        return pltpu.make_async_copy(blocks_hbm.at[t], blocks.at[t], blocks_sem.at[s])

    for s in range(td):
        load_blocks(s).start()

    barrier = pltpu.get_barrier_semaphore()
    mates = [sib, far, y_mate] + z_mates
    for mate in mates:
        pl.semaphore_signal(barrier, inc=1, device_id={"cols": mate}, device_id_type=MESH)
    pl.semaphore_wait(barrier, len(mates))

    def far_state(s):
        t = tile_at(td - 1 - s)
        return send(state.at[t], land.at[s], far_ssem.at[s], far_rsem.at[s], far)

    for s in range(td):
        far_state(s).start()
    sib_state = send(state, near.at[pl.ds(2 * td * par, td)], sib_ssem, sib_rsem, sib)
    sib_state.start()

    near[3 * td] = jnp.zeros(near.shape[1:], BF16)
    sums[pairs] = jnp.zeros(sums.shape[1:], F32)
    own_copy.wait()
    cot_copy.wait()
    sib_state.wait()
    far_base = 2 * td * par
    sib_base = 2 * td * (1 - par)

    acc[...] = jnp.zeros_like(acc)

    def weights(t):
        acc[0] += lax.dot_general(xs[t], pgs[t], TN, preferred_element_type=F32)
        acc[1] += lax.dot_general(cot[t], hs[t], TN, preferred_element_type=F32)

    def step(s, carry):
        t = tile_at(s)

        @pl.when(s > 0)
        def _():
            weights(tile_at(s - 1))

        far_state(s).wait()
        near[far_base + t] = land[s]

        @pl.when(s == td - 1)
        def _():
            pl.semaphore_signal(turn_sem, inc=1, device_id={"cols": sib}, device_id_type=MESH)

        load_blocks(s).wait()
        moved = mm(blocks[t, 0], near[table[s * slots]])
        for k in range(1, slots):
            moved += mm(blocks[t, k], near[table[s * slots + k]])
        moved = moved.astype(BF16)
        xs[t] = moved
        pre = mm(moved, w_in[...]) + bias[...]
        sig = jax.nn.sigmoid(pre)
        hs[t] = (pre * sig).astype(BF16)
        here = cot[t]
        back = lax.dot_general(here, w_out[...], NT, preferred_element_type=F32)
        pg = (back * sig * (1.0 + pre * (1.0 - sig))).astype(BF16)
        pgs[t] = pg
        up = here.astype(F32) + lax.dot_general(pg, w_in[...], NT, preferred_element_type=F32)
        up_t = jnp.transpose(up).astype(BF16)
        for k in range(slots):
            p = s * slots + k
            sums[p] = mm(up_t, blocks[t, k]) + sums[table[pairs + p]]
        return carry

    lax.fori_loop(0, td, step, 0)

    def far_part(i):
        return send(far_out.at[i], far_in.at[i], cfar_ssem.at[i], cfar_rsem.at[i], far)

    def sib_part(i):
        return send(sib_out.at[i], sib_in.at[i], csib_ssem.at[i], csib_rsem.at[i], sib)

    def post_far(i, carry):
        far_out[i] = sums[table[2 * pairs + far_base + i]].astype(BF16)
        far_part(i).start()
        return carry

    def post_sib(i, carry):
        sib_out[i] = sums[table[2 * pairs + sib_base + i]].astype(BF16)
        sib_part(i).start()
        return carry

    direct = lax.rem((low + 1) // 2, 2)
    most, more = td // 2 + td // 8, td - td // 8
    cuts = [0, td // 8, td // 4, td - (td - most) * direct, td - (td - more) * direct, td]
    pl.semaphore_wait(turn_sem, 1)
    lax.fori_loop(cuts[0], cuts[1], post_far, 0)
    weights(tile_at(td - 1))
    core_copy = send(acc.at[1 - par], core_in, core_sem.at[0], core_sem.at[1], sib)
    core_copy.start()
    lax.fori_loop(0, td, post_sib, 0)
    core_copy.wait()
    for z in range(nz):
        rows = pl.ds(z * rz, rz)
        piece = acc[par, rows] + core_in[rows]
        acc[par, rows] = piece
        z_out[z] = piece.astype(BF16)
    z_copies = []
    for d in range(1, nz):
        there = lax.rem(zi + d, nz)
        z_copies.append(
            send(z_out.at[there], z_in.at[d - 1], z_ssem.at[d - 1], z_rsem.at[d - 1], z_mates[d - 1])
        )
        z_copies[-1].start()
    lax.fori_loop(cuts[1], cuts[2], post_far, 0)
    total = acc[par, pl.ds(pl.multiple_of(zi * rz, rz), rz)]
    for d in range(1, nz):
        z_copies[d - 1].wait()
        total += z_in[d - 1].astype(F32)
    y_out[...] = total.astype(BF16)
    y_copy = send(y_out, y_in, y_sem.at[0], y_sem.at[1], y_mate)
    y_copy.start()
    lax.fori_loop(cuts[2], cuts[3], post_far, 0)
    y_copy.wait()
    gw[par, zi] = (y_out[...].astype(F32) + y_in[...].astype(F32)).astype(BF16)
    g_copies = []
    for d in range(1, nz):
        g_copies.append(
            send(gw.at[par, zi], gw.at[par, zi], g_ssem.at[d - 1], g_rsem.at[d - 1], z_mates[d - 1])
        )
        g_copies[-1].start()
    lax.fori_loop(cuts[3], cuts[4], post_far, 0)
    for g_copy in g_copies:
        g_copy.wait()
    last_copy = send(gw.at[par], gw.at[par], last_sem.at[0], last_sem.at[1], sib)
    last_copy.start()
    lax.fori_loop(cuts[4], cuts[5], post_far, 0)

    def out_copy(i):
        return pltpu.make_async_copy(out_buf.at[i], out_state.at[i], out_sem.at[i])

    def finish(i, carry):
        own = sums[table[2 * pairs + td + i]].astype(BF16).astype(F32)
        sib_part(i).wait()
        far_part(i).wait()
        whole = own + sib_in[i].astype(F32) + far_in[i].astype(F32)
        out_buf[i] = jnp.transpose(whole)
        out_copy(i).start()
        return carry

    lax.fori_loop(0, td, finish, 0)
    last_copy.wait()
    feat, hid = w_in.shape
    acc[0] = gw[0].reshape(feat, hid).astype(F32) * norm_scale
    w_in_copy = pltpu.make_async_copy(acc.at[0], out_w_in, local_sem.at[2])
    w_in_copy.start()
    turned[...] = jnp.transpose(gw[1].reshape(feat, hid).astype(F32) * norm_scale)
    w_out_copy = pltpu.make_async_copy(turned, out_w_out, local_sem.at[0])
    w_out_copy.start()
    for i in range(td):
        out_copy(i).wait()
    w_in_copy.wait()
    w_out_copy.wait()


def exchange(n, table, state, cotangent, blocks, w_in, bias, w_out):
    td, slots, cols, _ = blocks.shape
    feat = state.shape[2]
    hid = w_in.shape[1]
    nz = n // 4
    rz = feat // nz
    dma = pltpu.SemaphoreType.DMA
    vmem = pl.BlockSpec(memory_space=pltpu.VMEM)
    hbm = pl.BlockSpec(memory_space=pl.ANY)
    return pl.pallas_call(
        functools.partial(kernel, n),
        out_shape=(
            jax.ShapeDtypeStruct((td, cols, feat), F32),
            jax.ShapeDtypeStruct((feat, hid), F32),
            jax.ShapeDtypeStruct((hid, feat), F32),
        ),
        in_specs=[pl.BlockSpec(memory_space=pltpu.SMEM), hbm, hbm, hbm, vmem, vmem, vmem],
        out_specs=(hbm, hbm, hbm),
        scratch_shapes=[
            pltpu.VMEM((3 * td + 1, cols, feat), BF16),
            pltpu.VMEM((td, cols, feat), BF16),
            pltpu.VMEM((td, slots, cols, cols), BF16),
            pltpu.VMEM((td, cols, feat), BF16),
            pltpu.VMEM((td * slots + 1, feat, cols), F32),
            pltpu.VMEM((td, cols, feat), BF16),
            pltpu.VMEM((td, cols, hid), BF16),
            pltpu.VMEM((td, cols, hid), BF16),
            pltpu.VMEM((td, feat, cols), BF16),
            pltpu.VMEM((td, feat, cols), BF16),
            pltpu.VMEM((td, feat, cols), BF16),
            pltpu.VMEM((td, feat, cols), BF16),
            pltpu.VMEM((td, cols, feat), F32),
            pltpu.VMEM((2, feat, hid), F32),
            pltpu.VMEM((feat, hid), F32),
            pltpu.VMEM((nz, rz, hid), BF16),
            pltpu.VMEM((nz - 1, rz, hid), BF16),
            pltpu.VMEM((rz, hid), BF16),
            pltpu.VMEM((rz, hid), BF16),
            pltpu.VMEM((2, nz, rz, hid), BF16),
            pltpu.VMEM((hid, feat), F32),
            dma((3,)),
            dma((td,)),
            dma((td,)),
            dma((td,)),
            dma((td,)),
            dma,
            dma,
            dma((td,)),
            dma((td,)),
            dma((td,)),
            dma((td,)),
            dma((2,)),
            dma((nz - 1,)),
            dma((nz - 1,)),
            dma((2,)),
            dma((nz - 1,)),
            dma((nz - 1,)),
            dma((2,)),
            pltpu.SemaphoreType.REGULAR,
        ],
        compiler_params=pltpu.CompilerParams(
            collective_id=0, has_side_effects=True, vmem_limit_bytes=56 * 1024 * 1024
        ),
    )(table, state, cotangent, blocks, w_in, bias, w_out)


def per_device(state_field, cotangent, interp_blocks, upstream, src_counts, w_in, in_bias, w_out):
    td, cols, feat = state_field.shape
    slots = upstream.shape[1]
    n = lax.axis_size("cols")
    tile_total = td * n
    pairs = td * slots
    me = lax.axis_index("cols")
    live = jnp.arange(slots)[None, :] < src_counts[:, None]
    local = (upstream - me * td + td) % tile_total
    marked = jnp.where(live, local, -1)
    marked = jnp.where(me % 2 == 0, jnp.flip(marked, 0), marked).reshape(-1)
    order = jnp.arange(pairs, dtype=jnp.int32)
    same = (marked[:, None] == marked[None, :]) & (order[None, :] < order[:, None])
    before = jnp.max(jnp.where(same & (marked[:, None] >= 0), order[None, :], -1), axis=1)
    targets = jnp.arange(3 * td, dtype=jnp.int32)
    last = jnp.max(jnp.where(targets[:, None] == marked[None, :], order[None, :], -1), axis=1)
    table = jnp.concatenate(
        [
            jnp.where(marked < 0, 3 * td, marked),
            jnp.where(before < 0, pairs, before),
            jnp.where(last < 0, pairs, last),
        ]
    ).astype(jnp.int32)
    return exchange(
        n, table, state_field, cotangent, interp_blocks, w_in, in_bias[None, :], w_out
    )


def solution(mesh):
    placed = (
        P(("groups", "cols"), None, None),
        P(("groups", "cols"), None, None),
        P(("groups", "cols"), None, None, None),
        P(("groups", "cols"), None),
        P(("groups", "cols")),
        P(),
        P(),
        P(),
    )
    return jax.shard_map(
        per_device,
        mesh=mesh,
        in_specs=placed,
        out_specs=(P(("groups", "cols"), None, None), P("groups", None), P("groups", None)),
        check_vma=False,
    )
```

```python
import functools
import math

import jax
import jax.numpy as jnp
from jax import lax
from jax.experimental import pallas as pl
from jax.experimental.pallas import tpu as pltpu
from jax.sharding import PartitionSpec as P

F32 = jnp.float32
BF16 = jnp.bfloat16
MESH = pl.DeviceIdType.MESH
TN = (((0,), (0,)), ((), ()))
NT = (((1,), (1,)), ((), ()))


def mm(a, b):
    return jnp.dot(a, b, preferred_element_type=F32)


def kernel(
    n,
    table,
    state,
    cot_hbm,
    blocks_hbm,
    w_in,
    bias,
    w_out,
    out_state,
    out_w_in,
    out_w_out,
    near,
    land,
    blocks,
    cot,
    sums,
    xs,
    hs,
    pgs,
    far_out,
    sib_out,
    far_in,
    sib_in,
    out_buf,
    acc,
    core_in,
    z_out,
    z_in,
    y_out,
    y_in,
    gw,
    turned,
    local_sem,
    blocks_sem,
    out_sem,
    far_ssem,
    far_rsem,
    sib_ssem,
    sib_rsem,
    cfar_ssem,
    cfar_rsem,
    csib_ssem,
    csib_rsem,
    core_sem,
    z_ssem,
    z_rsem,
    y_sem,
    g_ssem,
    g_rsem,
    last_sem,
    turn_sem,
):
    td, slots = blocks.shape[0], blocks.shape[1]
    nz = z_out.shape[0]
    rz = z_out.shape[1]
    pairs = td * slots
    me = lax.axis_index("cols")
    par = lax.rem(me, 2)
    sib = me + 1 - 2 * par
    far = lax.rem(me - 1 + 2 * par + n, n)
    norm_scale = 1.0 / math.sqrt(n * td * blocks.shape[2])
    zi = me // 4
    low = lax.rem(me, 4)
    y_mate = me + 2 - 4 * (low // 2)
    z_mates = [lax.rem(zi + d, nz) * 4 + low for d in range(1, nz)]

    def tile_at(s):
        return par * s + (1 - par) * (td - 1 - s)

    def send(src, dst, ssem, rsem, to):
        return pltpu.make_async_remote_copy(
            src_ref=src,
            dst_ref=dst,
            send_sem=ssem,
            recv_sem=rsem,
            device_id={"cols": to},
            device_id_type=MESH,
        )

    own_copy = pltpu.make_async_copy(state, near.at[pl.ds(td, td)], local_sem.at[0])
    own_copy.start()
    cot_copy = pltpu.make_async_copy(cot_hbm, cot, local_sem.at[1])
    cot_copy.start()

    def load_blocks(s):
        t = tile_at(s)
        return pltpu.make_async_copy(blocks_hbm.at[t], blocks.at[t], blocks_sem.at[s])

    for s in range(td):
        load_blocks(s).start()

    barrier = pltpu.get_barrier_semaphore()
    mates = [sib, far, y_mate] + z_mates
    for mate in mates:
        pl.semaphore_signal(barrier, inc=1, device_id={"cols": mate}, device_id_type=MESH)
    pl.semaphore_wait(barrier, len(mates))

    def far_state(s):
        t = tile_at(td - 1 - s)
        return send(state.at[t], land.at[s], far_ssem.at[s], far_rsem.at[s], far)

    for s in range(td):
        far_state(s).start()
    sib_state = send(state, near.at[pl.ds(2 * td * par, td)], sib_ssem, sib_rsem, sib)
    sib_state.start()

    near[3 * td] = jnp.zeros(near.shape[1:], BF16)
    sums[pairs] = jnp.zeros(sums.shape[1:], F32)
    own_copy.wait()
    cot_copy.wait()
    sib_state.wait()
    far_base = 2 * td * par
    sib_base = 2 * td * (1 - par)

    acc[...] = jnp.zeros_like(acc)

    def weights(t):
        acc[0] += lax.dot_general(xs[t], pgs[t], TN, preferred_element_type=F32)
        acc[1] += lax.dot_general(cot[t], hs[t], TN, preferred_element_type=F32)

    def step(s, carry):
        t = tile_at(s)

        @pl.when(s > 0)
        def _():
            weights(tile_at(s - 1))

        far_state(s).wait()
        near[far_base + t] = land[s]

        @pl.when(s == td - 1)
        def _():
            pl.semaphore_signal(turn_sem, inc=1, device_id={"cols": sib}, device_id_type=MESH)

        load_blocks(s).wait()
        moved = mm(blocks[t, 0], near[table[s * slots]])
        for k in range(1, slots):
            moved += mm(blocks[t, k], near[table[s * slots + k]])
        moved = moved.astype(BF16)
        xs[t] = moved
        pre = mm(moved, w_in[...]) + bias[...]
        sig = jax.nn.sigmoid(pre)
        hs[t] = (pre * sig).astype(BF16)
        here = cot[t]
        back = lax.dot_general(here, w_out[...], NT, preferred_element_type=F32)
        pg = (back * sig * (1.0 + pre * (1.0 - sig))).astype(BF16)
        pgs[t] = pg
        up = here.astype(F32) + lax.dot_general(pg, w_in[...], NT, preferred_element_type=F32)
        up_t = jnp.transpose(up).astype(BF16)
        for k in range(slots):
            p = s * slots + k
            sums[p] = mm(up_t, blocks[t, k]) + sums[table[pairs + p]]
        return carry

    lax.fori_loop(0, td, step, 0)

    def far_part(i):
        return send(far_out.at[i], far_in.at[i], cfar_ssem.at[i], cfar_rsem.at[i], far)

    def sib_part(i):
        return send(sib_out.at[i], sib_in.at[i], csib_ssem.at[i], csib_rsem.at[i], sib)

    def post_far(i, carry):
        far_out[i] = sums[table[2 * pairs + far_base + i]].astype(BF16)
        far_part(i).start()
        return carry

    def post_sib(i, carry):
        sib_out[i] = sums[table[2 * pairs + sib_base + i]].astype(BF16)
        sib_part(i).start()
        return carry

    direct = lax.rem((low + 1) // 2, 2)
    most = td // 2 + td // 8
    cuts = [0, td // 8, td // 4, td - (td - most) * direct]
    pl.semaphore_wait(turn_sem, 1)
    lax.fori_loop(cuts[0], cuts[1], post_far, 0)
    weights(tile_at(td - 1))
    core_copy = send(acc.at[1 - par], core_in, core_sem.at[0], core_sem.at[1], sib)
    core_copy.start()
    lax.fori_loop(0, td, post_sib, 0)
    core_copy.wait()
    for z in range(nz):
        rows = pl.ds(z * rz, rz)
        piece = acc[par, rows] + core_in[rows]
        acc[par, rows] = piece
        z_out[z] = piece.astype(BF16)
    z_copies = []
    for d in range(1, nz):
        there = lax.rem(zi + d, nz)
        z_copies.append(
            send(z_out.at[there], z_in.at[d - 1], z_ssem.at[d - 1], z_rsem.at[d - 1], z_mates[d - 1])
        )
        z_copies[-1].start()
    lax.fori_loop(cuts[1], cuts[2], post_far, 0)
    total = acc[par, pl.ds(pl.multiple_of(zi * rz, rz), rz)]
    for d in range(1, nz):
        z_copies[d - 1].wait()
        total += z_in[d - 1].astype(F32)
    y_out[...] = total.astype(BF16)
    y_copy = send(y_out, y_in, y_sem.at[0], y_sem.at[1], y_mate)
    y_copy.start()
    lax.fori_loop(cuts[2], cuts[3], post_far, 0)
    y_copy.wait()
    gw[par, zi] = (y_out[...].astype(F32) + y_in[...].astype(F32)).astype(BF16)
    g_copies = []
    for d in range(1, nz):
        g_copies.append(
            send(gw.at[par, zi], gw.at[par, zi], g_ssem.at[d - 1], g_rsem.at[d - 1], z_mates[d - 1])
        )
        g_copies[-1].start()
    lax.fori_loop(cuts[3], td, post_far, 0)

    def out_copy(i):
        return pltpu.make_async_copy(out_buf.at[i], out_state.at[i], out_sem.at[i])

    def finish(i, carry):
        own = sums[table[2 * pairs + td + i]].astype(BF16).astype(F32)
        sib_part(i).wait()
        far_part(i).wait()
        whole = own + sib_in[i].astype(F32) + far_in[i].astype(F32)
        out_buf[i] = jnp.transpose(whole)
        out_copy(i).start()
        return carry

    lax.fori_loop(0, td // 2, finish, 0)
    for g_copy in g_copies:
        g_copy.wait()
    last_copy = send(gw.at[par], gw.at[par], last_sem.at[0], last_sem.at[1], sib)
    last_copy.start()
    lax.fori_loop(td // 2, td, finish, 0)
    last_copy.wait()
    feat, hid = w_in.shape
    acc[0] = gw[0].reshape(feat, hid).astype(F32) * norm_scale
    w_in_copy = pltpu.make_async_copy(acc.at[0], out_w_in, local_sem.at[2])
    w_in_copy.start()
    turned[...] = jnp.transpose(gw[1].reshape(feat, hid).astype(F32) * norm_scale)
    w_out_copy = pltpu.make_async_copy(turned, out_w_out, local_sem.at[0])
    w_out_copy.start()
    for i in range(td):
        out_copy(i).wait()
    w_in_copy.wait()
    w_out_copy.wait()


def exchange(n, table, state, cotangent, blocks, w_in, bias, w_out):
    td, slots, cols, _ = blocks.shape
    feat = state.shape[2]
    hid = w_in.shape[1]
    nz = n // 4
    rz = feat // nz
    dma = pltpu.SemaphoreType.DMA
    vmem = pl.BlockSpec(memory_space=pltpu.VMEM)
    hbm = pl.BlockSpec(memory_space=pl.ANY)
    return pl.pallas_call(
        functools.partial(kernel, n),
        out_shape=(
            jax.ShapeDtypeStruct((td, cols, feat), F32),
            jax.ShapeDtypeStruct((feat, hid), F32),
            jax.ShapeDtypeStruct((hid, feat), F32),
        ),
        in_specs=[pl.BlockSpec(memory_space=pltpu.SMEM), hbm, hbm, hbm, vmem, vmem, vmem],
        out_specs=(hbm, hbm, hbm),
        scratch_shapes=[
            pltpu.VMEM((3 * td + 1, cols, feat), BF16),
            pltpu.VMEM((td, cols, feat), BF16),
            pltpu.VMEM((td, slots, cols, cols), BF16),
            pltpu.VMEM((td, cols, feat), BF16),
            pltpu.VMEM((td * slots + 1, feat, cols), F32),
            pltpu.VMEM((td, cols, feat), BF16),
            pltpu.VMEM((td, cols, hid), BF16),
            pltpu.VMEM((td, cols, hid), BF16),
            pltpu.VMEM((td, feat, cols), BF16),
            pltpu.VMEM((td, feat, cols), BF16),
            pltpu.VMEM((td, feat, cols), BF16),
            pltpu.VMEM((td, feat, cols), BF16),
            pltpu.VMEM((td, cols, feat), F32),
            pltpu.VMEM((2, feat, hid), F32),
            pltpu.VMEM((feat, hid), F32),
            pltpu.VMEM((nz, rz, hid), BF16),
            pltpu.VMEM((nz - 1, rz, hid), BF16),
            pltpu.VMEM((rz, hid), BF16),
            pltpu.VMEM((rz, hid), BF16),
            pltpu.VMEM((2, nz, rz, hid), BF16),
            pltpu.VMEM((hid, feat), F32),
            dma((3,)),
            dma((td,)),
            dma((td,)),
            dma((td,)),
            dma((td,)),
            dma,
            dma,
            dma((td,)),
            dma((td,)),
            dma((td,)),
            dma((td,)),
            dma((2,)),
            dma((nz - 1,)),
            dma((nz - 1,)),
            dma((2,)),
            dma((nz - 1,)),
            dma((nz - 1,)),
            dma((2,)),
            pltpu.SemaphoreType.REGULAR,
        ],
        compiler_params=pltpu.CompilerParams(
            collective_id=0, has_side_effects=True, vmem_limit_bytes=56 * 1024 * 1024
        ),
    )(table, state, cotangent, blocks, w_in, bias, w_out)


def per_device(state_field, cotangent, interp_blocks, upstream, src_counts, w_in, in_bias, w_out):
    td, cols, feat = state_field.shape
    slots = upstream.shape[1]
    n = lax.axis_size("cols")
    tile_total = td * n
    pairs = td * slots
    me = lax.axis_index("cols")
    live = jnp.arange(slots)[None, :] < src_counts[:, None]
    local = (upstream - me * td + td) % tile_total
    marked = jnp.where(live, local, -1)
    marked = jnp.where(me % 2 == 0, jnp.flip(marked, 0), marked).reshape(-1)
    order = jnp.arange(pairs, dtype=jnp.int32)
    same = (marked[:, None] == marked[None, :]) & (order[None, :] < order[:, None])
    before = jnp.max(jnp.where(same & (marked[:, None] >= 0), order[None, :], -1), axis=1)
    targets = jnp.arange(3 * td, dtype=jnp.int32)
    last = jnp.max(jnp.where(targets[:, None] == marked[None, :], order[None, :], -1), axis=1)
    table = jnp.concatenate(
        [
            jnp.where(marked < 0, 3 * td, marked),
            jnp.where(before < 0, pairs, before),
            jnp.where(last < 0, pairs, last),
        ]
    ).astype(jnp.int32)
    return exchange(
        n, table, state_field, cotangent, interp_blocks, w_in, in_bias[None, :], w_out
    )


def solution(mesh):
    placed = (
        P(("groups", "cols"), None, None),
        P(("groups", "cols"), None, None),
        P(("groups", "cols"), None, None, None),
        P(("groups", "cols"), None),
        P(("groups", "cols")),
        P(),
        P(),
        P(),
    )
    return jax.shard_map(
        per_device,
        mesh=mesh,
        in_specs=placed,
        out_specs=(P(("groups", "cols"), None, None), P("groups", None), P("groups", None)),
        check_vma=False,
    )
```
